128 devices in a mesh: dp: 16 (over y, x), fsdp: 8 (over z, core).
Axes of the slice: x: 4, y: 4, z: 4, core: 2. Of those that a mesh axis runs over, the one named last changes fastest.
Arguments:
- block_input: bfloat16 [2, 16384, 1024], P(None, ('dp', 'fsdp')), may hold values from -6 to 6
- seq_start: int32 [2, 16384], P(None, ('dp', 'fsdp')), may hold values from 0 to 15871, as said below
- norm_gain: bfloat16 [1024], P('fsdp'), may hold values from 0.099609375 to 1.8984375
- in_weight: bfloat16 [1024, 3072], P('fsdp'), may hold values from -0.1875 to 0.1875
- conv_weight: bfloat16 [3, 1024], P(None, 'fsdp'), may hold values from -3.5 to 3.5
- out_weight: bfloat16 [1024, 1024], P('fsdp'), may hold values from -0.1875 to 0.1875
- ffn_gain: bfloat16 [1024], P('fsdp'), may hold values from 0.099609375 to 1.8984375
- gate_weight: bfloat16 [1024, 4608], P('fsdp'), may hold values from -0.1875 to 0.1875
- up_weight: bfloat16 [1024, 4608], P('fsdp'), may hold values from -0.1875 to 0.1875
- down_weight: bfloat16 [4608, 1024], P('fsdp'), may hold values from -0.125 to 0.125
- cotangent: bfloat16 [2, 16384, 1024], P(None, ('dp', 'fsdp')), may hold values from -24 to 24
Outputs:
- block_output: bfloat16 [2, 16384, 1024], P(None, ('dp', 'fsdp'))
- input_grad: float32 [2, 16384, 1024], P(None, ('dp', 'fsdp'))
- norm_gain_grad: float32 [1024], P('fsdp')
- in_weight_grad: float32 [1024, 3072], P('fsdp')
- conv_weight_grad: float32 [3, 1024], P(None, 'fsdp')
- out_weight_grad: float32 [1024, 1024], P('fsdp')
- ffn_gain_grad: float32 [1024], P('fsdp')
- gate_weight_grad: float32 [1024, 4608], P('fsdp')
- up_weight_grad: float32 [1024, 4608], P('fsdp')
- down_weight_grad: float32 [4608, 1024], P('fsdp')
The draws below stay inside these ranges and needn't reach their ends.
Inputs may be any that keep to these rules, and one draw needn't show every extreme that they name: seq_start is the index within the micro-batch of the first token of the token's sequence; it never falls along a micro-batch, the first sequence starts at 0, and every sequence holds between 512 and 1536 tokens.
All inputs are finite; a program needn't handle non-finite values.
Results may differ from the reference program's by a relative error of at most 0.018.
Values may be sent and summed in bfloat16 or wider, within the bound.
No kernel may reach another device: no remote copies, remote signals or barrier semaphores. Data moves between devices by JAX's collectives and lax.ppermute only.
A program may use at most 256 MiB of HBM per device.

```python
import jax
import jax.numpy as jnp
from jax import lax

D = 1024
FF = 4608
KW = 3
MICRO = 2
SEQ_LEN = 1024
TOKENS = 16384


def draw_seq_start(key, part):
    key = jax.random.fold_in(key, 7)
    count = TOKENS // SEQ_LEN
    order = jnp.arange(count, dtype=jnp.int32)
    offsets = jax.random.randint(key, (MICRO, count), 0, SEQ_LEN // 2, dtype=jnp.int32)
    micro_index = jnp.arange(MICRO, dtype=jnp.int32)
    forced = (micro_index[:, None] == 0) & (order[None, :] == count - 1)
    offsets = jnp.where(forced, SEQ_LEN // 2 - 1, offsets)
    cuts = jnp.where(order[None, :] == 0, 0, order[None, :] * SEQ_LEN + offsets)
    position = jnp.arange(TOKENS, dtype=jnp.int32)
    chosen = jnp.where(cuts[:, None, :] <= position[None, :, None], cuts[:, None, :], 0)
    return jnp.max(chosen, -1).astype(jnp.int32)


def raised(drawn, rng, source, target, blocks, factor):
    def block_of(axis_at):
        return (jnp.arange(drawn.shape[axis_at]) // (drawn.shape[axis_at] // blocks)).reshape((-1,) + (1,) * (drawn.ndim - 1 - axis_at))

    first = jax.random.permutation(rng, blocks)[block_of(target)]
    second = (block_of(target) + blocks // 2) % blocks
    return jnp.where((block_of(source) == first) | (block_of(source) == second), factor * drawn, drawn)


def block_levels(own_key, extent, shards, low, high):
    loudness = 1.0
    for axis_at, parts in shards:
        heights = jax.random.uniform(jax.random.fold_in(jax.random.fold_in(own_key, 6), axis_at), (parts,), jnp.float32, low / len(shards), high / len(shards))
        loudness = loudness * jnp.repeat(jnp.exp(heights), extent[axis_at] // parts).reshape((-1,) + (1,) * (len(extent) - 1 - axis_at))
    return loudness


def scatter_about(stream_key, dims, width, most, split=(), kind=jnp.bfloat16):
    values = width * jax.random.normal(stream_key, dims, jnp.float32)
    if split:
        values = values * block_levels(stream_key, dims, split, -0.22, 0.18)
    return jnp.clip(values, -most, most).astype(kind)


def gaussian_with(rng, dims, scale, bound, split, heavy, kind=jnp.bfloat16):
    drawn = scale * jax.random.normal(rng, dims, jnp.float32)
    if split:
        drawn = drawn * block_levels(rng, dims, split, -0.22, 0.18)
    return jnp.clip(raised(drawn, jax.random.fold_in(rng, 3), *heavy), -bound, bound).astype(kind)


def setup_inputs(seed: int = 0) -> dict:
    arg_keys = jax.random.split(jax.random.key(seed), 12)
    return {
        "block_input": scatter_about(arg_keys[0], (MICRO, TOKENS, D), 1.0, 6.0, ((1, 128),)),
        "seq_start": draw_seq_start(jax.random.fold_in(arg_keys[11], 71), 0),
        "norm_gain": jnp.clip(1.0 + 0.18 * jax.random.normal(arg_keys[2], (D,), jnp.float32), 0.099609375, 1.8984375).astype(jnp.bfloat16),
        "in_weight": scatter_about(arg_keys[3], (D, 3 * D), D ** -0.5, 0.1875, ((0, 8),)),
        "conv_weight": scatter_about(arg_keys[4], (KW, D), KW ** -0.5, 3.5, ((1, 8),)),
        "out_weight": scatter_about(arg_keys[5], (D, D), D ** -0.5, 0.1875, ((0, 8),)),
        "ffn_gain": jnp.clip(1.0 + 0.18 * jax.random.normal(arg_keys[6], (D,), jnp.float32), 0.099609375, 1.8984375).astype(jnp.bfloat16),
        "gate_weight": scatter_about(arg_keys[7], (D, FF), D ** -0.5, 0.1875, ((0, 8),)),
        "up_weight": scatter_about(arg_keys[8], (D, FF), D ** -0.5, 0.1875, ((0, 8),)),
        "down_weight": scatter_about(arg_keys[9], (FF, D), (FF // 2) ** -0.5, 0.125, ((0, 8),)),
        "cotangent": gaussian_with(arg_keys[10], (MICRO, TOKENS, D), 1.0, 24.0, ((1, 128),), (1, 2, 128, 5.5)),
    }


EPS = 1e-05
HIGH = lax.Precision.HIGHEST

@jax.custom_vjp
def low(v):
    return lax.optimization_barrier(v.astype(jnp.bfloat16)).astype(jnp.float32)

@jax.custom_vjp
def low_back(v):
    return v

def low_keep(v):
    return (low(v), None)

def low_pass(kept, grad):
    return (grad,)

def back_keep(v):
    return (v, None)

def back_low(kept, grad):
    return (low(grad),)
low.defvjp(low_keep, low_pass)
low_back.defvjp(back_keep, back_low)

def block(block_input, starts, norm_gain, in_weight, conv_weight, out_weight, ffn_gain, gate_weight, up_weight, down_weight):
    inv_one = lax.rsqrt(lax.optimization_barrier(jnp.mean(block_input * block_input, -1, keepdims=True)) + EPS)
    normed_one = low(block_input * inv_one * norm_gain)
    projected = low_back(jnp.dot(normed_one, in_weight, precision=HIGH))
    b_part = projected[:, :D]
    c_part = projected[:, D:2 * D]
    x_part = projected[:, 2 * D:]
    mixed = b_part * x_part
    position = jnp.arange(TOKENS, dtype=jnp.int32)
    conv_out = jnp.zeros((TOKENS, D), jnp.float32)
    for tap_index in range(KW):
        shifted = jnp.concatenate([jnp.zeros((tap_index, D), jnp.float32), mixed[:TOKENS - tap_index]], 0)
        valid = (position - tap_index >= starts).astype(jnp.float32)[:, None]
        conv_out = conv_out + conv_weight[tap_index] * shifted * valid
    gated = low(c_part * conv_out)
    resid = block_input + low_back(jnp.dot(gated, out_weight, precision=HIGH))
    inv_two = lax.rsqrt(lax.optimization_barrier(jnp.mean(resid * resid, -1, keepdims=True)) + EPS)
    normed_two = low(resid * inv_two * ffn_gain)
    gate_pre = low_back(jnp.dot(normed_two, gate_weight, precision=HIGH))
    up_pre = low_back(jnp.dot(normed_two, up_weight, precision=HIGH))
    hidden = low(jax.nn.silu(gate_pre) * up_pre)
    return resid + low_back(jnp.dot(hidden, down_weight, precision=HIGH))

def reference(block_input, seq_start, norm_gain, in_weight, conv_weight, out_weight, ffn_gain, gate_weight, up_weight, down_weight, cotangent):
    weights = tuple((w.astype(jnp.float32) for w in (norm_gain, in_weight, conv_weight, out_weight, ffn_gain, gate_weight, up_weight, down_weight)))

    def one_micro(totals, item):
        inputs, starts, grad_out = item

        def apply(inputs_f, *params):
            return block(inputs_f, starts, *params)
        result, pull = jax.vjp(apply, inputs.astype(jnp.float32), *weights)
        grads = pull(grad_out.astype(jnp.float32))
        totals = tuple((a + b for a, b in zip(totals, grads[1:])))
        return (totals, (result.astype(jnp.bfloat16), grads[0]))
    zeros = tuple((jnp.zeros_like(w) for w in weights))
    totals, stacked = lax.scan(one_micro, zeros, (block_input, seq_start, cotangent))
    return (stacked[0], stacked[1], totals[0], totals[1], totals[2], totals[3], totals[4], totals[5], totals[6], totals[7])
```

```python
import jax
import jax.numpy as jnp
from jax import lax
from jax.sharding import Mesh, PartitionSpec as P

KW = 3
EPS = 1e-05
GROUP = ("z", "core")
EVERY = ("y", "x", "z", "core")
CONTRACT = (((0,), (0,)), ((), ()))
BACK_DIMS = (((1,), (1,)), ((), ()))
F32 = jnp.float32
BF16 = jnp.bfloat16


def dot(a, b, dims=(((1,), (0,)), ((), ()))):
    return lax.dot_general(a, b, dims, preferred_element_type=F32)


def shift(value, axis, distance):
    size = lax.axis_size(axis)
    return lax.ppermute(value, axis, [(i, (i + distance) % size) for i in range(size)])


def from_behind(block, distance):
    size = lax.axis_size(EVERY)
    route = [(i - distance, i) for i in range(size) if 0 <= i - distance < size]
    return lax.ppermute(block, EVERY, route)


def fetch(value, axis):
    return [value] + [shift(value, axis, d) for d in range(1, lax.axis_size(axis))]


def place(pieces, axis, dim, dtype):
    size = lax.axis_size(axis)
    here = lax.axis_index(axis)
    width = pieces[0].shape[dim]
    shape = list(pieces[0].shape)
    shape[dim] = width * size
    out = jnp.zeros(shape, dtype)
    for d, piece in enumerate(pieces):
        start = lax.rem(here - d + size, size) * width
        out = lax.dynamic_update_slice_in_dim(out, piece.astype(dtype), start, dim)
    return out


def gather(value, axis, dim, dtype=BF16):
    return place(fetch(value, axis), axis, dim, dtype)


def scatter_sum(value, axis, dim):
    size = lax.axis_size(axis)
    here = lax.axis_index(axis)
    width = value.shape[dim] // size

    def block(d):
        start = lax.rem(here + d, size) * width
        return lax.dynamic_slice_in_dim(value, start, width, dim)

    total = block(0).astype(F32)
    for d in range(1, size):
        total = total + shift(block(d).astype(BF16), axis, d).astype(F32)
    return total


def give_back(partial, axis):
    size = lax.axis_size(axis)
    rows = partial.shape[0] // size
    total = partial[:rows]
    for d in range(1, size):
        part = partial[d * rows : (d + 1) * rows].astype(BF16)
        total = total + shift(part, axis, -d).astype(F32)
    return total


def shards(
    block_input,
    seq_start,
    norm_gain,
    in_weight,
    conv_weight,
    out_weight,
    ffn_gain,
    gate_weight,
    up_weight,
    down_weight,
    cotangent,
):
    micro, rows, width = block_input.shape
    owned = norm_gain.shape[0]
    hidden_width = gate_weight.shape[1]
    n_x = lax.axis_size("x")
    n_group = lax.axis_size(GROUP)
    x_here = lax.axis_index("x")
    tokens = micro * rows

    grad_low = cotangent.reshape(tokens, width)
    grad_moved = jnp.concatenate(fetch(grad_low, "x"), 0)

    branch_weight = lax.all_gather(
        jnp.concatenate([in_weight, out_weight], 1), GROUP, axis=0, tiled=True
    )
    gains = lax.all_gather(
        jnp.concatenate(
            [norm_gain[None], ffn_gain[None], conv_weight, jnp.zeros((3, owned), BF16)], 0
        ),
        GROUP,
        axis=1,
        tiled=True,
    ).astype(F32)
    in_full = branch_weight[:, : 3 * width]
    out_full = branch_weight[:, 3 * width :]
    gain_one = gains[0]
    gain_two = gains[1]
    conv_taps = gains[2 : 2 + KW]

    piece = hidden_width // (n_group * n_x)
    share = piece * n_group

    def quarter(weight):
        split = weight.reshape(owned, n_group, n_x, piece)
        return lax.dynamic_index_in_dim(split, x_here, 2, False).reshape(owned, share)

    wide = lax.all_gather(
        jnp.concatenate([quarter(gate_weight), quarter(up_weight)], 1), GROUP, axis=0, tiled=True
    )
    down = lax.all_gather(
        lax.dynamic_slice_in_dim(down_weight, x_here * piece, piece, 0), GROUP, axis=0, tiled=True
    )

    inputs = block_input.reshape(tokens, width).astype(F32)
    inv_one = lax.rsqrt(jnp.mean(inputs * inputs, -1, keepdims=True) + EPS)
    normed_one = (inputs * inv_one * gain_one).astype(BF16)
    projected = dot(normed_one, in_full)
    b_part = projected[:, :width]
    c_part = projected[:, width : 2 * width]
    x_part = projected[:, 2 * width :]
    mixed = (b_part * x_part).reshape(micro, rows, width)
    rim = from_behind(mixed[:, rows - (KW - 1) :], 1)
    extended = jnp.concatenate([rim, mixed], 1)
    position = lax.axis_index(EVERY) * rows + lax.iota(jnp.int32, rows)
    masks = [(position[None] - k >= seq_start).astype(F32)[:, :, None] for k in range(KW)]
    conv_out = jnp.zeros_like(mixed)
    for k in range(KW):
        low = KW - 1 - k
        conv_out = conv_out + conv_taps[k] * extended[:, low : low + rows] * masks[k]
    conv_out = conv_out.reshape(tokens, width)
    gated = (c_part * conv_out).astype(BF16)
    resid = inputs + dot(gated, out_full)
    inv_two = lax.rsqrt(jnp.mean(resid * resid, -1, keepdims=True) + EPS)
    normed_two = (resid * inv_two * gain_two).astype(BF16)

    moved = jnp.concatenate(fetch(normed_two, "x"), 0)
    pre = dot(moved, wide)
    gate_pre = pre[:, :share]
    up_pre = pre[:, share:]
    sigma = jax.nn.sigmoid(gate_pre)
    hidden = (gate_pre * sigma * up_pre).astype(BF16)
    grad_hidden = dot(grad_moved, down, BACK_DIMS)
    grad_gate = (grad_hidden * up_pre * sigma * (1.0 + gate_pre * (1.0 - sigma))).astype(BF16)
    grad_up = (grad_hidden * gate_pre * sigma).astype(BF16)
    grad_wide = jnp.concatenate([grad_gate, grad_up], 1)
    grad_normed = give_back(dot(grad_wide, wide, BACK_DIMS), "x")
    result = (resid + give_back(dot(hidden, down), "x")).astype(BF16)
    wide_term = dot(moved, grad_wide, CONTRACT).astype(BF16)
    down_term = dot(hidden, grad_moved, CONTRACT).astype(BF16)
    wide_sum = lax.psum_scatter(wide_term, GROUP, scatter_dimension=0, tiled=True)
    down_sum = lax.psum_scatter(down_term, GROUP, scatter_dimension=0, tiled=True)

    grad_out = grad_low.astype(F32)
    ffn_term = jnp.sum(grad_normed * resid * inv_two, 0)
    hat_two = grad_normed * gain_two
    grad_resid = (
        grad_out
        + inv_two * hat_two
        - resid * inv_two**3 * jnp.mean(hat_two * resid, -1, keepdims=True)
    )
    grad_branch = grad_resid.astype(BF16)
    out_term = dot(gated, grad_branch, CONTRACT)
    grad_gated = dot(grad_branch, out_full, BACK_DIMS)
    grad_c = grad_gated * conv_out
    grad_conv = (grad_gated * c_part).reshape(micro, rows, width)
    tap_terms = []
    grad_extended = jnp.zeros_like(extended)
    for k in range(KW):
        low = KW - 1 - k
        masked = grad_conv * masks[k]
        tap_terms.append(jnp.sum(masked * extended[:, low : low + rows], (0, 1)))
        grad_extended = grad_extended + jnp.pad(
            masked * conv_taps[k], ((0, 0), (low, k), (0, 0))
        )
    incoming = from_behind(grad_extended[:, : KW - 1], -1)
    grad_mixed = grad_extended[:, KW - 1 :] + jnp.pad(
        incoming, ((0, 0), (rows - (KW - 1), 0), (0, 0))
    )
    grad_mixed = grad_mixed.reshape(tokens, width)
    grad_projected = jnp.concatenate([grad_mixed * x_part, grad_c, grad_mixed * b_part], 1).astype(
        BF16
    )
    in_term = dot(normed_one, grad_projected, CONTRACT)
    grad_first = dot(grad_projected, in_full, BACK_DIMS)
    norm_term = jnp.sum(grad_first * inputs * inv_one, 0)
    hat_one = grad_first * gain_one
    grad_input = (
        grad_resid
        + inv_one * hat_one
        - inputs * inv_one**3 * jnp.mean(hat_one * inputs, -1, keepdims=True)
    )

    small = jnp.pad(jnp.stack([norm_term, ffn_term] + tap_terms, 0), ((0, 123), (0, 0)))
    branch_term = jnp.concatenate(
        [in_term.astype(BF16), out_term.astype(BF16), small.T.astype(BF16)], 1
    )
    branch_sum = lax.psum_scatter(branch_term, GROUP, scatter_dimension=0, tiled=True)
    branch_sum = scatter_sum(scatter_sum(branch_sum, "y", 0), "x", 0).astype(BF16)
    branch_sum = gather(gather(branch_sum, "x", 0), "y", 0, F32)
    in_grad = branch_sum[:, : 3 * width]
    out_grad = branch_sum[:, 3 * width : 4 * width]
    gain_grads = branch_sum[:, 4 * width : 4 * width + 2 + KW].T

    wide_sum = gather(scatter_sum(wide_sum, "y", 0).astype(BF16), "y", 0)
    down_sum = gather(scatter_sum(down_sum, "y", 1).astype(BF16), "y", 1)
    wide_all = gather(wide_sum.reshape(1, owned, 2, n_group, piece), "x", 0)
    wide_all = wide_all.transpose(2, 1, 3, 0, 4).reshape(2, owned, hidden_width).astype(F32)
    down_grad = gather(down_sum, "x", 0, F32)
    return (
        result.reshape(micro, rows, width),
        grad_input.reshape(micro, rows, width),
        gain_grads[0],
        in_grad,
        gain_grads[2:],
        out_grad,
        gain_grads[1],
        wide_all[0],
        wide_all[1],
        down_grad,
    )


def solution(mesh):
    fine = Mesh(mesh.devices.reshape(4, 4, 4, 2), EVERY)
    token = P(None, EVERY, None)
    owner = P(GROUP, None)
    return jax.shard_map(
        shards,
        mesh=fine,
        in_specs=(
            token,
            P(None, EVERY),
            P(GROUP),
            owner,
            P(None, GROUP),
            owner,
            P(GROUP),
            owner,
            owner,
            owner,
            token,
        ),
        out_specs=(
            token,
            token,
            P(GROUP),
            owner,
            P(None, GROUP),
            owner,
            P(GROUP),
            owner,
            owner,
            owner,
        ),
        check_vma=False,
    )
```

```python
import jax
import jax.numpy as jnp
from jax import lax
from jax.experimental import pallas as pl
from jax.experimental.pallas import tpu as pltpu
from jax.sharding import Mesh, PartitionSpec as P

KW = 3
EPS = 1e-05
GROUP = ("z", "core")
EVERY = ("y", "x", "z", "core")
GROUP_SIZE = 8
CONTRACT = (((0,), (0,)), ((), ()))
BACK_DIMS = (((1,), (1,)), ((), ()))
F32 = jnp.float32
BF16 = jnp.bfloat16


def dot(a, b, dims=(((1,), (0,)), ((), ()))):
    return lax.dot_general(a, b, dims, preferred_element_type=F32)


def shift(value, axis, distance):
    size = lax.axis_size(axis)
    return lax.ppermute(value, axis, [(i, (i + distance) % size) for i in range(size)])


def from_behind(block, distance):
    size = lax.axis_size(EVERY)
    route = [(i - distance, i) for i in range(size) if 0 <= i - distance < size]
    return lax.ppermute(block, EVERY, route)


def fetch(value, axis):
    return [value] + [shift(value, axis, d) for d in range(1, lax.axis_size(axis))]


def place(pieces, axis, dim, dtype):
    size = lax.axis_size(axis)
    here = lax.axis_index(axis)
    width = pieces[0].shape[dim]
    shape = list(pieces[0].shape)
    shape[dim] = width * size
    out = jnp.zeros(shape, dtype)
    for d, piece in enumerate(pieces):
        start = lax.rem(here - d + size, size) * width
        out = lax.dynamic_update_slice_in_dim(out, piece.astype(dtype), start, dim)
    return out


def gather(value, axis, dim, dtype=BF16):
    return place(fetch(value, axis), axis, dim, dtype)


def scatter_sum(value, axis, dim):
    size = lax.axis_size(axis)
    here = lax.axis_index(axis)
    width = value.shape[dim] // size

    def block(d):
        start = lax.rem(here + d, size) * width
        return lax.dynamic_slice_in_dim(value, start, width, dim)

    total = block(0).astype(F32)
    for d in range(1, size):
        total = total + shift(block(d).astype(BF16), axis, d).astype(F32)
    return total


def term_kernel(*refs):
    count = (len(refs) - 2) // 2
    lefts, rights = refs[:count], refs[count : 2 * count]
    out, turned = refs[2 * count :]
    rows = lefts[0].shape[0]

    @pl.when(pl.program_id(0) == 0)
    def _():
        for i, left in enumerate(lefts):
            turned[:, i * rows : (i + 1) * rows] = left[...].T

    total = dot(turned[:, :rows], rights[0][...])
    for i in range(1, count):
        total = total + dot(turned[:, i * rows : (i + 1) * rows], rights[i][...])
    out[...] = total.astype(out.dtype)


def weight_term(lefts, rights, tile, skip, tiles):
    rows, tall = lefts[0].shape
    wide = tile * tiles
    count = len(lefts)
    return pl.pallas_call(
        term_kernel,
        grid=(tiles,),
        in_specs=[pl.BlockSpec((rows, tall), lambda i: (0, 0))] * count
        + [pl.BlockSpec((rows, tile), lambda i: (0, i + skip))] * count,
        out_specs=pl.BlockSpec((tall, tile), lambda i: (0, i)),
        out_shape=jax.ShapeDtypeStruct((tall, wide), BF16),
        scratch_shapes=[pltpu.VMEM((tall, rows * count), BF16)],
        compiler_params=pltpu.CompilerParams(
            vmem_limit_bytes=16 * 1024 * 1024, dimension_semantics=("arbitrary",)
        ),
        cost_estimate=pl.CostEstimate(
            flops=2 * count * rows * tall * wide,
            bytes_accessed=2 * (count * rows * (tall + wide) + tall * wide),
            transcendentals=0,
        ),
    )(*lefts, *rights)


def unpack_kernel(source, gate, up, down):
    n_y, n_x, strip, _ = source.shape
    rows = n_y * strip
    n_group = GROUP_SIZE
    share = gate.shape[1] // n_x
    piece = share // n_group
    width = down.shape[1]
    for half, out in enumerate((gate, up)):
        for j in range(n_group):
            low = half * share + j * piece
            for y in range(n_y):
                parts = [source[y, x, :, low : low + piece].astype(F32) for x in range(n_x)]
                out[
                    y * strip : (y + 1) * strip, j * n_x * piece : (j + 1) * n_x * piece
                ] = jnp.concatenate(parts, 1)
    rest = piece - rows
    for x in range(n_x):
        top = x * piece
        for y in range(n_y):
            main = source[y, x, :, 2 * share : 2 * share + width]
            down[top + y * strip : top + (y + 1) * strip] = main.astype(F32)
        for q in range(rows // rest):
            y, low = divmod(q * rest, strip)
            block = source[y, x, low : low + rest, 2 * share + width :]
            down[top + rows : top + piece, q * 128 : (q + 1) * 128] = block.astype(F32)


def unpack(source, hidden_width, width):
    n_y, n_x, strip, packed = source.shape
    rows = n_y * strip
    shapes = [(rows, hidden_width), (rows, hidden_width), (hidden_width // GROUP_SIZE, width)]
    return pl.pallas_call(
        unpack_kernel,
        out_shape=[jax.ShapeDtypeStruct(shape, F32) for shape in shapes],
        compiler_params=pltpu.CompilerParams(vmem_limit_bytes=20 * 1024 * 1024),
        cost_estimate=pl.CostEstimate(
            flops=0, bytes_accessed=6 * n_x * rows * packed, transcendentals=0
        ),
    )(source)


def after(value, *others):
    return lax.optimization_barrier((value, others))[0]


def block_of(value, axis, distance, dim):
    size = lax.axis_size(axis)
    width = value.shape[dim] // size
    start = lax.rem(lax.axis_index(axis) + distance, size) * width
    return lax.dynamic_slice_in_dim(value, start, width, dim)


def relay(strip):
    stacked = place([piece[None] for piece in fetch(strip, "z")], "z", 0, BF16)
    joined = place(fetch(stacked, "y"), "y", 2, BF16)
    return fetch(joined, "core"), stacked


def shards(
    block_input,
    seq_start,
    norm_gain,
    in_weight,
    conv_weight,
    out_weight,
    ffn_gain,
    gate_weight,
    up_weight,
    down_weight,
    cotangent,
):
    micro, rows, width = block_input.shape
    owned, hidden_width = gate_weight.shape
    n_x = lax.axis_size("x")
    x_here = lax.axis_index("x")
    tokens = micro * rows
    share = hidden_width // n_x
    piece = share // GROUP_SIZE

    columns = jnp.pad(
        jnp.concatenate([norm_gain[None], ffn_gain[None], conv_weight], 0), ((0, 128 - 2 - KW), (0, 0))
    ).T
    in_full = lax.all_gather(
        jnp.concatenate([in_weight, out_weight, columns], 1), GROUP, axis=0, tiled=True
    )
    cores, stacked = relay(block_of(block_of(down_weight, "x", 0, 0), "y", 0, 1))

    grad_low = cotangent.reshape(tokens, width)
    grad_moved = fetch(grad_low, "x")
    input_moved = fetch(after(block_input.reshape(tokens, width), grad_moved), "x")

    def quarter(weight):
        split = weight.reshape(owned, GROUP_SIZE, n_x, piece)
        return lax.dynamic_index_in_dim(split, x_here, 2, False).reshape(owned, share)

    wide = lax.all_gather(
        after(
            jnp.concatenate([quarter(gate_weight), quarter(up_weight)], 1), stacked, grad_moved, input_moved
        ),
        GROUP,
        axis=0,
        tiled=True,
    )

    gains = in_full[:, 4 * width :].T.astype(F32)
    gain_one = gains[0]
    gain_two = gains[1]
    conv_taps = gains[2 : 2 + KW]
    out_full = in_full[:, 3 * width : 4 * width]
    in_full = in_full[:, : 3 * width]
    inputs = block_input.reshape(tokens, width).astype(F32)

    def norm_of(value):
        inverse = lax.rsqrt(jnp.mean(value * value, -1, keepdims=True) + EPS)
        return inverse, (value * inverse * gain_one).astype(BF16)

    inv_one, normed_one = norm_of(inputs)
    projected = dot(normed_one, in_full)
    b_part = projected[:, :width]
    c_part = projected[:, width : 2 * width]
    x_part = projected[:, 2 * width :]
    mixed = (b_part * x_part).reshape(micro, rows, width)
    rim = from_behind(mixed[:, rows - (KW - 1) :], 1)
    extended = jnp.concatenate([rim, mixed], 1)
    position = lax.axis_index(EVERY) * rows + lax.iota(jnp.int32, rows)
    masks = [(position[None] - k >= seq_start).astype(F32)[:, :, None] for k in range(KW)]
    conv_out = jnp.zeros_like(mixed)
    for k in range(KW):
        low = KW - 1 - k
        conv_out = conv_out + conv_taps[k] * extended[:, low : low + rows] * masks[k]
    conv_out = conv_out.reshape(tokens, width)
    gated = (c_part * conv_out).astype(BF16)
    resid = inputs + dot(gated, out_full)
    inv_two = lax.rsqrt(jnp.mean(resid * resid, -1, keepdims=True) + EPS)
    normed_two = (resid * inv_two * gain_two).astype(BF16)

    down = place([part[:, None] for part in cores], "core", 1, BF16).reshape(-1, width)

    moved = fetch(normed_two, "x")
    hidden = [None] * n_x
    grad_wide = [None] * n_x
    grad_back = [None] * n_x
    for d in (1, 2, 3, 0):
        pre = dot(moved[d], wide)
        gate_pre = pre[:, :share]
        up_pre = pre[:, share:]
        sigma = jax.nn.sigmoid(gate_pre)
        hidden[d] = (gate_pre * sigma * up_pre).astype(BF16)
        grad_hidden = dot(grad_moved[d], down, BACK_DIMS)
        grad_gate = (grad_hidden * up_pre * sigma * (1.0 + gate_pre * (1.0 - sigma))).astype(BF16)
        grad_up = (grad_hidden * gate_pre * sigma).astype(BF16)
        grad_wide[d] = jnp.concatenate([grad_gate, grad_up], 1)
        grad_back[d] = dot(grad_wide[d], wide, BACK_DIMS)
    grad_normed = grad_back[0]
    for d in (1, 3, 2):
        grad_normed = grad_normed + shift(grad_back[d].astype(BF16), "x", -d).astype(F32)

    moved, grad_wide, hidden, term_grads = after(
        (moved, grad_wide, hidden, grad_moved), grad_back
    )
    wide_term = weight_term(moved, grad_wide, 384, 0, 2 * share // 384)
    down_term = weight_term(hidden, term_grads, 512, 0, width // 512)
    gated_moved = fetch(after(gated, grad_normed), "x")
    wide_term, down_term, gated_moved = after((wide_term, down_term, gated_moved), gated_moved)
    down_term = down_term.reshape(GROUP_SIZE, piece, width)
    rest = down_term[:, owned:].reshape(GROUP_SIZE, piece - owned, width // 128, 128)
    ffn_term = jnp.concatenate(
        [
            wide_term,
            down_term[:, :owned].reshape(-1, width),
            rest.swapaxes(1, 2).reshape(-1, 128),
        ],
        1,
    )
    grad_normed = after(grad_normed, ffn_term)
    ffn_sum = lax.psum_scatter(ffn_term, GROUP, scatter_dimension=0, tiled=True)

    grad_out = grad_low.astype(F32)
    ffn_gain_term = jnp.sum(grad_normed * resid * inv_two, 0)
    hat_two = grad_normed * gain_two
    grad_resid = (
        grad_out
        + inv_two * hat_two
        - resid * inv_two**3 * jnp.mean(hat_two * resid, -1, keepdims=True)
    )
    grad_branch = grad_resid.astype(BF16)
    grad_gated = dot(grad_branch, out_full, BACK_DIMS)
    grad_c = grad_gated * conv_out
    grad_conv = (grad_gated * c_part).reshape(micro, rows, width)
    tap_terms = []
    grad_extended = jnp.zeros_like(extended)
    for k in range(KW):
        low = KW - 1 - k
        masked = grad_conv * masks[k]
        tap_terms.append(jnp.sum(masked * extended[:, low : low + rows], (0, 1)))
        grad_extended = grad_extended + jnp.pad(
            masked * conv_taps[k], ((0, 0), (low, k), (0, 0))
        )
    incoming = from_behind(grad_extended[:, : KW - 1], -1)
    grad_mixed = grad_extended[:, KW - 1 :] + jnp.pad(
        incoming, ((0, 0), (rows - (KW - 1), 0), (0, 0))
    )
    grad_mixed = grad_mixed.reshape(tokens, width)
    grad_projected = jnp.concatenate([grad_mixed * x_part, grad_c, grad_mixed * b_part], 1).astype(
        BF16
    )

    def columns_of(d):
        return jnp.concatenate(
            [block_of(grad_projected, "x", d, 1), block_of(grad_branch, "x", d, 1)], 1
        )

    taken = [columns_of(0)] + [shift(columns_of(d), "x", d) for d in range(1, n_x)]
    ffn_sum = scatter_sum(ffn_sum, "y", 0).astype(BF16)
    grad_first = dot(grad_projected, in_full, BACK_DIMS)
    norm_term = jnp.sum(grad_first * inputs * inv_one, 0)
    hat_one = grad_first * gain_one
    grad_input = (
        grad_resid
        + inv_one * hat_one
        - inputs * inv_one**3 * jnp.mean(hat_one * inputs, -1, keepdims=True)
    )
    normed_moved = [normed_one] + [
        norm_of(value.astype(F32))[1] for value in input_moved[1:]
    ]
    in_part = 3 * width // n_x
    out_part = width // n_x
    in_term = weight_term(normed_moved, taken, out_part, 0, 3)
    out_term = weight_term(gated_moved, taken, out_part, 3, 1)
    small = jnp.pad(
        jnp.stack([norm_term, ffn_gain_term] + tap_terms, 0), ((0, 128 - 2 - KW), (0, 0))
    )
    branch_term = jnp.concatenate([in_term, out_term, small.T.astype(BF16)], 1)
    branch_sum = branch_term.reshape(lax.axis_size("z"), 2, owned, -1)
    branch_sum = scatter_sum(branch_sum, "core", 1).astype(BF16)
    branch_sum, ffn_sum = after((branch_sum, ffn_sum), ffn_sum)
    ffn_sum = lax.all_gather(ffn_sum, ("y", "x"), axis=0)
    branch_sum = scatter_sum(branch_sum, "z", 0)
    branch_sum = branch_sum.astype(BF16).reshape(owned, -1)

    ffn_sum = ffn_sum.reshape(lax.axis_size("y"), n_x, *ffn_sum.shape[1:])
    gate_grad, up_grad, down_grad = unpack(ffn_sum, hidden_width, width)

    branch_sum = gather(scatter_sum(branch_sum, "y", 0).astype(BF16), "y", 0)
    parts = fetch(branch_sum, "x")

    hidden = after(hidden, taken)
    block_parts = [resid + dot(hidden[0], down)]
    for d in (1, 3, 2):
        block_parts.append(shift(dot(hidden[d], down).astype(BF16), "x", -d))
    block_parts = after(block_parts, parts)
    block_out = sum(part.astype(F32) for part in block_parts)
    result = block_out.astype(BF16)

    in_grad = place([part[:, :in_part] for part in parts], "x", 1, F32)
    out_grad = place([part[:, in_part : in_part + out_part] for part in parts], "x", 1, F32)
    gain_grads = sum(part[:, in_part + out_part :].astype(F32) for part in parts).T
    return (
        result.reshape(micro, rows, width),
        grad_input.reshape(micro, rows, width),
        gain_grads[0],
        in_grad,
        gain_grads[2 : 2 + KW],
        out_grad,
        gain_grads[1],
        gate_grad,
        up_grad,
        down_grad,
    )


def solution(mesh):
    fine = Mesh(mesh.devices.reshape(4, 4, 4, 2), EVERY)
    token = P(None, EVERY, None)
    owner = P(GROUP, None)
    return jax.shard_map(
        shards,
        mesh=fine,
        in_specs=(
            token,
            P(None, EVERY),
            P(GROUP),
            owner,
            P(None, GROUP),
            owner,
            P(GROUP),
            owner,
            owner,
            owner,
            token,
        ),
        out_specs=(
            token,
            token,
            P(GROUP),
            owner,
            P(None, GROUP),
            owner,
            P(GROUP),
            owner,
            owner,
            owner,
        ),
        check_vma=False,
    )
```

```python
import jax
import jax.numpy as jnp
from jax import lax
from jax.experimental import pallas as pl
from jax.experimental.pallas import tpu as pltpu
from jax.sharding import Mesh, PartitionSpec as P

KW = 3
EPS = 1e-05
GROUP = ("z", "core")
EVERY = ("y", "x", "z", "core")
GROUP_SIZE = 8
CONTRACT = (((0,), (0,)), ((), ()))
BACK_DIMS = (((1,), (1,)), ((), ()))
F32 = jnp.float32
BF16 = jnp.bfloat16


def dot(a, b, dims=(((1,), (0,)), ((), ()))):
    return lax.dot_general(a, b, dims, preferred_element_type=F32)


def shift(value, axis, distance):
    size = lax.axis_size(axis)
    return lax.ppermute(value, axis, [(i, (i + distance) % size) for i in range(size)])


def from_behind(block, distance):
    size = lax.axis_size(EVERY)
    route = [(i - distance, i) for i in range(size) if 0 <= i - distance < size]
    return lax.ppermute(block, EVERY, route)


def fetch(value, axis):
    return [value] + [shift(value, axis, d) for d in range(1, lax.axis_size(axis))]


def place(pieces, axis, dim, dtype):
    size = lax.axis_size(axis)
    here = lax.axis_index(axis)
    width = pieces[0].shape[dim]
    shape = list(pieces[0].shape)
    shape[dim] = width * size
    out = jnp.zeros(shape, dtype)
    for d, piece in enumerate(pieces):
        start = lax.rem(here - d + size, size) * width
        out = lax.dynamic_update_slice_in_dim(out, piece.astype(dtype), start, dim)
    return out


def gather(value, axis, dim, dtype=BF16):
    return place(fetch(value, axis), axis, dim, dtype)


def scatter_sum(value, axis, dim):
    size = lax.axis_size(axis)
    here = lax.axis_index(axis)
    width = value.shape[dim] // size

    def block(d):
        start = lax.rem(here + d, size) * width
        return lax.dynamic_slice_in_dim(value, start, width, dim)

    total = block(0).astype(F32)
    for d in range(1, size):
        total = total + shift(block(d).astype(BF16), axis, d).astype(F32)
    return total


def term_kernel(*refs):
    count = (len(refs) - 2) // 2
    lefts, rights = refs[:count], refs[count : 2 * count]
    out, turned = refs[2 * count :]
    rows = lefts[0].shape[0]

    @pl.when(pl.program_id(0) == 0)
    def _():
        for i, left in enumerate(lefts):
            turned[:, i * rows : (i + 1) * rows] = left[...].T

    total = dot(turned[:, :rows], rights[0][...])
    for i in range(1, count):
        total = total + dot(turned[:, i * rows : (i + 1) * rows], rights[i][...])
    out[...] = total.astype(out.dtype)


def weight_term(lefts, rights, tile, skip, tiles):
    rows, tall = lefts[0].shape
    wide = tile * tiles
    count = len(lefts)
    return pl.pallas_call(
        term_kernel,
        grid=(tiles,),
        in_specs=[pl.BlockSpec((rows, tall), lambda i: (0, 0))] * count
        + [pl.BlockSpec((rows, tile), lambda i: (0, i + skip))] * count,
        out_specs=pl.BlockSpec((tall, tile), lambda i: (0, i)),
        out_shape=jax.ShapeDtypeStruct((tall, wide), BF16),
        scratch_shapes=[pltpu.VMEM((tall, rows * count), BF16)],
        compiler_params=pltpu.CompilerParams(
            vmem_limit_bytes=16 * 1024 * 1024, dimension_semantics=("arbitrary",)
        ),
        cost_estimate=pl.CostEstimate(
            flops=2 * count * rows * tall * wide,
            bytes_accessed=2 * (count * rows * (tall + wide) + tall * wide),
            transcendentals=0,
        ),
    )(*lefts, *rights)


def unpack_kernel(source, gate, up, down):
    n_y, n_x, strip, _ = source.shape
    rows = n_y * strip
    n_group = GROUP_SIZE
    share = gate.shape[1] // n_x
    piece = share // n_group
    width = down.shape[1]
    for half, out in enumerate((gate, up)):
        for j in range(n_group):
            low = half * share + j * piece
            for y in range(n_y):
                parts = [source[y, x, :, low : low + piece].astype(F32) for x in range(n_x)]
                out[
                    y * strip : (y + 1) * strip, j * n_x * piece : (j + 1) * n_x * piece
                ] = jnp.concatenate(parts, 1)
    rest = piece - rows
    for x in range(n_x):
        top = x * piece
        for y in range(n_y):
            main = source[y, x, :, 2 * share : 2 * share + width]
            down[top + y * strip : top + (y + 1) * strip] = main.astype(F32)
        for q in range(rows // rest):
            y, low = divmod(q * rest, strip)
            block = source[y, x, low : low + rest, 2 * share + width :]
            down[top + rows : top + piece, q * 128 : (q + 1) * 128] = block.astype(F32)


def unpack(source, hidden_width, width):
    n_y, n_x, strip, packed = source.shape
    rows = n_y * strip
    shapes = [(rows, hidden_width), (rows, hidden_width), (hidden_width // GROUP_SIZE, width)]
    return pl.pallas_call(
        unpack_kernel,
        out_shape=[jax.ShapeDtypeStruct(shape, F32) for shape in shapes],
        compiler_params=pltpu.CompilerParams(vmem_limit_bytes=20 * 1024 * 1024),
        cost_estimate=pl.CostEstimate(
            flops=0, bytes_accessed=6 * n_x * rows * packed, transcendentals=0
        ),
    )(source)


def after(value, *others):
    return lax.optimization_barrier((value, others))[0]


def block_of(value, axis, distance, dim):
    size = lax.axis_size(axis)
    width = value.shape[dim] // size
    start = lax.rem(lax.axis_index(axis) + distance, size) * width
    return lax.dynamic_slice_in_dim(value, start, width, dim)


def shards(
    block_input,
    seq_start,
    norm_gain,
    in_weight,
    conv_weight,
    out_weight,
    ffn_gain,
    gate_weight,
    up_weight,
    down_weight,
    cotangent,
):
    micro, rows, width = block_input.shape
    owned, hidden_width = gate_weight.shape
    n_x = lax.axis_size("x")
    x_here = lax.axis_index("x")
    tokens = micro * rows
    share = hidden_width // n_x
    piece = share // GROUP_SIZE

    columns = jnp.pad(
        jnp.concatenate([norm_gain[None], ffn_gain[None], conv_weight], 0), ((0, 128 - 2 - KW), (0, 0))
    ).T
    in_full = lax.all_gather(
        jnp.concatenate([in_weight, out_weight, columns], 1), GROUP, axis=0, tiled=True
    )
    grad_low = cotangent.reshape(tokens, width)
    grad_moved = fetch(grad_low, "x")
    input_moved = fetch(after(block_input.reshape(tokens, width), grad_moved), "x")

    def quarter(weight):
        split = weight.reshape(owned, GROUP_SIZE, n_x, piece)
        return lax.dynamic_index_in_dim(split, x_here, 2, False).reshape(owned, share)

    down_piece = block_of(down_weight, "x", 0, 0)
    down_rest = down_piece[owned:].reshape(piece - owned, width // 128, 128)
    packed = jnp.concatenate(
        [
            quarter(gate_weight),
            quarter(up_weight),
            down_piece[:owned],
            down_rest.swapaxes(0, 1).reshape(-1, 128),
        ],
        1,
    )
    packed = lax.all_gather(
        after(packed, in_full, grad_moved, input_moved), GROUP, axis=0, tiled=True
    )
    wide = packed[:, : 2 * share]
    down = packed[:, 2 * share : 2 * share + width].reshape(GROUP_SIZE, owned, width)
    down_rest = packed[:, 2 * share + width :].reshape(
        GROUP_SIZE, width // 128, piece - owned, 128
    )
    down_rest = down_rest.swapaxes(1, 2).reshape(GROUP_SIZE, piece - owned, width)
    down = jnp.concatenate([down, down_rest], 1).reshape(-1, width)

    gains = in_full[:, 4 * width :].T.astype(F32)
    gain_one = gains[0]
    gain_two = gains[1]
    conv_taps = gains[2 : 2 + KW]
    out_full = in_full[:, 3 * width : 4 * width]
    in_full = in_full[:, : 3 * width]
    inputs = block_input.reshape(tokens, width).astype(F32)

    def norm_of(value):
        inverse = lax.rsqrt(jnp.mean(value * value, -1, keepdims=True) + EPS)
        return inverse, (value * inverse * gain_one).astype(BF16)

    inv_one, normed_one = norm_of(inputs)
    projected = dot(normed_one, in_full)
    b_part = projected[:, :width]
    c_part = projected[:, width : 2 * width]
    x_part = projected[:, 2 * width :]
    mixed = (b_part * x_part).reshape(micro, rows, width)
    rim = from_behind(mixed[:, rows - (KW - 1) :], 1)
    extended = jnp.concatenate([rim, mixed], 1)
    position = lax.axis_index(EVERY) * rows + lax.iota(jnp.int32, rows)
    masks = [(position[None] - k >= seq_start).astype(F32)[:, :, None] for k in range(KW)]
    conv_out = jnp.zeros_like(mixed)
    for k in range(KW):
        low = KW - 1 - k
        conv_out = conv_out + conv_taps[k] * extended[:, low : low + rows] * masks[k]
    conv_out = conv_out.reshape(tokens, width)
    gated = (c_part * conv_out).astype(BF16)
    resid = inputs + dot(gated, out_full)
    inv_two = lax.rsqrt(jnp.mean(resid * resid, -1, keepdims=True) + EPS)
    normed_two = (resid * inv_two * gain_two).astype(BF16)

    moved = fetch(normed_two, "x")
    hidden = [None] * n_x
    grad_wide = [None] * n_x
    grad_back = [None] * n_x
    for d in (1, 2, 3, 0):
        pre = dot(moved[d], wide)
        gate_pre = pre[:, :share]
        up_pre = pre[:, share:]
        sigma = jax.nn.sigmoid(gate_pre)
        hidden[d] = (gate_pre * sigma * up_pre).astype(BF16)
        grad_hidden = dot(grad_moved[d], down, BACK_DIMS)
        grad_gate = (grad_hidden * up_pre * sigma * (1.0 + gate_pre * (1.0 - sigma))).astype(BF16)
        grad_up = (grad_hidden * gate_pre * sigma).astype(BF16)
        grad_wide[d] = jnp.concatenate([grad_gate, grad_up], 1)
        grad_back[d] = dot(grad_wide[d], wide, BACK_DIMS)
    grad_normed = grad_back[0]
    for d in (1, 3, 2):
        grad_normed = grad_normed + shift(grad_back[d].astype(BF16), "x", -d).astype(F32)

    moved, grad_wide, hidden, term_grads = after(
        (moved, grad_wide, hidden, grad_moved), grad_back
    )
    wide_term = weight_term(moved, grad_wide, 384, 0, 2 * share // 384)
    down_term = weight_term(hidden, term_grads, 512, 0, width // 512)
    gated_moved = fetch(after(gated, grad_normed), "x")
    wide_term, down_term, gated_moved = after((wide_term, down_term, gated_moved), gated_moved)
    down_term = down_term.reshape(GROUP_SIZE, piece, width)
    rest = down_term[:, owned:].reshape(GROUP_SIZE, piece - owned, width // 128, 128)
    ffn_term = jnp.concatenate(
        [
            wide_term,
            down_term[:, :owned].reshape(-1, width),
            rest.swapaxes(1, 2).reshape(-1, 128),
        ],
        1,
    )
    grad_normed = after(grad_normed, ffn_term)
    ffn_sum = lax.psum_scatter(ffn_term, GROUP, scatter_dimension=0, tiled=True)

    grad_out = grad_low.astype(F32)
    ffn_gain_term = jnp.sum(grad_normed * resid * inv_two, 0)
    hat_two = grad_normed * gain_two
    grad_resid = (
        grad_out
        + inv_two * hat_two
        - resid * inv_two**3 * jnp.mean(hat_two * resid, -1, keepdims=True)
    )
    grad_branch = grad_resid.astype(BF16)
    grad_gated = dot(grad_branch, out_full, BACK_DIMS)
    grad_c = grad_gated * conv_out
    grad_conv = (grad_gated * c_part).reshape(micro, rows, width)
    tap_terms = []
    grad_extended = jnp.zeros_like(extended)
    for k in range(KW):
        low = KW - 1 - k
        masked = grad_conv * masks[k]
        tap_terms.append(jnp.sum(masked * extended[:, low : low + rows], (0, 1)))
        grad_extended = grad_extended + jnp.pad(
            masked * conv_taps[k], ((0, 0), (low, k), (0, 0))
        )
    incoming = from_behind(grad_extended[:, : KW - 1], -1)
    grad_mixed = grad_extended[:, KW - 1 :] + jnp.pad(
        incoming, ((0, 0), (rows - (KW - 1), 0), (0, 0))
    )
    grad_mixed = grad_mixed.reshape(tokens, width)
    grad_projected = jnp.concatenate([grad_mixed * x_part, grad_c, grad_mixed * b_part], 1).astype(
        BF16
    )

    def columns_of(d):
        return jnp.concatenate(
            [block_of(grad_projected, "x", d, 1), block_of(grad_branch, "x", d, 1)], 1
        )

    taken = [columns_of(0)] + [shift(columns_of(d), "x", d) for d in range(1, n_x)]
    ffn_sum = scatter_sum(ffn_sum, "y", 0).astype(BF16)
    hidden = after(hidden, grad_projected)
    block_parts = [resid + dot(hidden[0], down)]
    for d in range(1, n_x):
        block_parts.append(dot(hidden[d], down).astype(BF16))
    taken, block_parts = after((taken, block_parts), block_parts)
    grad_first = dot(grad_projected, in_full, BACK_DIMS)
    norm_term = jnp.sum(grad_first * inputs * inv_one, 0)
    hat_one = grad_first * gain_one
    grad_input = (
        grad_resid
        + inv_one * hat_one
        - inputs * inv_one**3 * jnp.mean(hat_one * inputs, -1, keepdims=True)
    )
    normed_moved = [normed_one] + [
        norm_of(value.astype(F32))[1] for value in input_moved[1:]
    ]
    in_part = 3 * width // n_x
    out_part = width // n_x
    in_term = weight_term(normed_moved, taken, out_part, 0, 3)
    out_term = weight_term(gated_moved, taken, out_part, 3, 1)
    small = jnp.pad(
        jnp.stack([norm_term, ffn_gain_term] + tap_terms, 0), ((0, 128 - 2 - KW), (0, 0))
    )
    branch_term = jnp.concatenate([in_term, out_term, small.T.astype(BF16)], 1)
    branch_sum = branch_term.reshape(lax.axis_size("z"), 2, owned, -1)
    branch_sum = scatter_sum(branch_sum, "core", 1).astype(BF16)
    branch_sum, ffn_sum = after((branch_sum, ffn_sum), ffn_sum)
    ffn_sum = lax.all_gather(ffn_sum, ("y", "x"), axis=0)
    branch_sum = scatter_sum(branch_sum, "z", 0)
    block_parts = block_parts[:1] + [
        shift(block_parts[d], "x", -d) for d in range(1, n_x)
    ]
    branch_sum, block_parts = after((branch_sum, block_parts), block_parts)
    branch_sum = branch_sum.astype(BF16).reshape(owned, -1)

    ffn_sum = ffn_sum.reshape(lax.axis_size("y"), n_x, *ffn_sum.shape[1:])
    gate_grad, up_grad, down_grad = unpack(ffn_sum, hidden_width, width)

    branch_sum = gather(scatter_sum(branch_sum, "y", 0).astype(BF16), "y", 0)
    parts = fetch(branch_sum, "x")

    block_out = sum(part.astype(F32) for part in block_parts)
    result = block_out.astype(BF16)

    in_grad = place([part[:, :in_part] for part in parts], "x", 1, F32)
    out_grad = place([part[:, in_part : in_part + out_part] for part in parts], "x", 1, F32)
    gain_grads = sum(part[:, in_part + out_part :].astype(F32) for part in parts).T
    return (
        result.reshape(micro, rows, width),
        grad_input.reshape(micro, rows, width),
        gain_grads[0],
        in_grad,
        gain_grads[2 : 2 + KW],
        out_grad,
        gain_grads[1],
        gate_grad,
        up_grad,
        down_grad,
    )


def solution(mesh):
    fine = Mesh(mesh.devices.reshape(4, 4, 4, 2), EVERY)
    token = P(None, EVERY, None)
    owner = P(GROUP, None)
    return jax.shard_map(
        shards,
        mesh=fine,
        in_specs=(
            token,
            P(None, EVERY),
            P(GROUP),
            owner,
            P(None, GROUP),
            owner,
            P(GROUP),
            owner,
            owner,
            owner,
            token,
        ),
        out_specs=(
            token,
            token,
            P(GROUP),
            owner,
            P(None, GROUP),
            owner,
            P(GROUP),
            owner,
            owner,
            owner,
        ),
        check_vma=False,
    )
```

```python
import jax
import jax.numpy as jnp
from jax import lax
from jax.experimental import pallas as pl
from jax.experimental.pallas import tpu as pltpu
from jax.sharding import Mesh, PartitionSpec as P

KW = 3
EPS = 1e-05
GROUP = ("z", "core")
EVERY = ("y", "x", "z", "core")
GROUP_SIZE = 8
CONTRACT = (((0,), (0,)), ((), ()))
BACK_DIMS = (((1,), (1,)), ((), ()))
F32 = jnp.float32
BF16 = jnp.bfloat16


def dot(a, b, dims=(((1,), (0,)), ((), ()))):
    return lax.dot_general(a, b, dims, preferred_element_type=F32)


def shift(value, axis, distance):
    size = lax.axis_size(axis)
    return lax.ppermute(value, axis, [(i, (i + distance) % size) for i in range(size)])


def from_behind(block, distance):
    size = lax.axis_size(EVERY)
    route = [(i - distance, i) for i in range(size) if 0 <= i - distance < size]
    return lax.ppermute(block, EVERY, route)


def fetch(value, axis):
    return [value] + [shift(value, axis, d) for d in range(1, lax.axis_size(axis))]


def place(pieces, axis, dim, dtype):
    size = lax.axis_size(axis)
    here = lax.axis_index(axis)
    width = pieces[0].shape[dim]
    shape = list(pieces[0].shape)
    shape[dim] = width * size
    out = jnp.zeros(shape, dtype)
    for d, piece in enumerate(pieces):
        start = lax.rem(here - d + size, size) * width
        out = lax.dynamic_update_slice_in_dim(out, piece.astype(dtype), start, dim)
    return out


def gather(value, axis, dim, dtype=BF16):
    return place(fetch(value, axis), axis, dim, dtype)


def scatter_sum(value, axis, dim):
    size = lax.axis_size(axis)
    here = lax.axis_index(axis)
    width = value.shape[dim] // size

    def block(d):
        start = lax.rem(here + d, size) * width
        return lax.dynamic_slice_in_dim(value, start, width, dim)

    total = block(0).astype(F32)
    for d in range(1, size):
        total = total + shift(block(d).astype(BF16), axis, d).astype(F32)
    return total


def term_kernel(*refs):
    count = (len(refs) - 2) // 2
    lefts, rights = refs[:count], refs[count : 2 * count]
    out, turned = refs[2 * count :]
    rows = lefts[0].shape[0]

    @pl.when(pl.program_id(0) == 0)
    def _():
        for i, left in enumerate(lefts):
            turned[:, i * rows : (i + 1) * rows] = left[...].T

    total = dot(turned[:, :rows], rights[0][...])
    for i in range(1, count):
        total = total + dot(turned[:, i * rows : (i + 1) * rows], rights[i][...])
    out[...] = total.astype(out.dtype)


def weight_term(lefts, rights, tile, skip, tiles):
    rows, tall = lefts[0].shape
    wide = tile * tiles
    count = len(lefts)
    return pl.pallas_call(
        term_kernel,
        grid=(tiles,),
        in_specs=[pl.BlockSpec((rows, tall), lambda i: (0, 0))] * count
        + [pl.BlockSpec((rows, tile), lambda i: (0, i + skip))] * count,
        out_specs=pl.BlockSpec((tall, tile), lambda i: (0, i)),
        out_shape=jax.ShapeDtypeStruct((tall, wide), BF16),
        scratch_shapes=[pltpu.VMEM((tall, rows * count), BF16)],
        compiler_params=pltpu.CompilerParams(
            vmem_limit_bytes=16 * 1024 * 1024, dimension_semantics=("arbitrary",)
        ),
        cost_estimate=pl.CostEstimate(
            flops=2 * count * rows * tall * wide,
            bytes_accessed=2 * (count * rows * (tall + wide) + tall * wide),
            transcendentals=0,
        ),
    )(*lefts, *rights)


def unpack_kernel(source, gate, up, down):
    n_y, n_x, strip, _ = source.shape
    rows = n_y * strip
    n_group = GROUP_SIZE
    share = gate.shape[1] // n_x
    piece = share // n_group
    width = down.shape[1]
    for half, out in enumerate((gate, up)):
        for j in range(n_group):
            low = half * share + j * piece
            for y in range(n_y):
                parts = [source[y, x, :, low : low + piece].astype(F32) for x in range(n_x)]
                out[
                    y * strip : (y + 1) * strip, j * n_x * piece : (j + 1) * n_x * piece
                ] = jnp.concatenate(parts, 1)
    rest = piece - rows
    for x in range(n_x):
        top = x * piece
        for y in range(n_y):
            main = source[y, x, :, 2 * share : 2 * share + width]
            down[top + y * strip : top + (y + 1) * strip] = main.astype(F32)
        for q in range(rows // rest):
            y, low = divmod(q * rest, strip)
            block = source[y, x, low : low + rest, 2 * share + width :]
            down[top + rows : top + piece, q * 128 : (q + 1) * 128] = block.astype(F32)


def unpack(source, hidden_width, width):
    n_y, n_x, strip, packed = source.shape
    rows = n_y * strip
    shapes = [(rows, hidden_width), (rows, hidden_width), (hidden_width // GROUP_SIZE, width)]
    return pl.pallas_call(
        unpack_kernel,
        out_shape=[jax.ShapeDtypeStruct(shape, F32) for shape in shapes],
        compiler_params=pltpu.CompilerParams(vmem_limit_bytes=20 * 1024 * 1024),
        cost_estimate=pl.CostEstimate(
            flops=0, bytes_accessed=6 * n_x * rows * packed, transcendentals=0
        ),
    )(source)


def after(value, *others):
    return lax.optimization_barrier((value, others))[0]


def block_of(value, axis, distance, dim):
    size = lax.axis_size(axis)
    width = value.shape[dim] // size
    start = lax.rem(lax.axis_index(axis) + distance, size) * width
    return lax.dynamic_slice_in_dim(value, start, width, dim)


def shards(
    block_input,
    seq_start,
    norm_gain,
    in_weight,
    conv_weight,
    out_weight,
    ffn_gain,
    gate_weight,
    up_weight,
    down_weight,
    cotangent,
):
    micro, rows, width = block_input.shape
    owned, hidden_width = gate_weight.shape
    n_x = lax.axis_size("x")
    x_here = lax.axis_index("x")
    tokens = micro * rows
    share = hidden_width // n_x
    piece = share // GROUP_SIZE

    columns = jnp.pad(
        jnp.concatenate([norm_gain[None], ffn_gain[None], conv_weight], 0), ((0, 128 - 2 - KW), (0, 0))
    ).T
    in_full = lax.all_gather(
        jnp.concatenate([in_weight, out_weight, columns], 1), GROUP, axis=0, tiled=True
    )
    down_strip = block_of(block_of(down_weight, "x", 0, 0), "y", 0, 1)
    joined = place([part[None] for part in fetch(down_strip, "z")], "z", 0, BF16)
    joined = place(fetch(joined, "y"), "y", 2, BF16)

    grad_low = cotangent.reshape(tokens, width)
    grad_moved = fetch(grad_low, "x")
    input_moved = fetch(block_input.reshape(tokens, width), "x")

    def quarter(weight):
        split = weight.reshape(owned, GROUP_SIZE, n_x, piece)
        return lax.dynamic_index_in_dim(split, x_here, 2, False).reshape(owned, share)

    wide = jnp.concatenate([quarter(gate_weight), quarter(up_weight)], 1)
    wide = lax.all_gather(
        after(wide, in_full, joined, grad_moved, input_moved), GROUP, axis=0, tiled=True
    )
    cores = fetch(joined, "core")
    down = place([part[:, None] for part in cores], "core", 1, BF16).reshape(-1, width)

    gains = in_full[:, 4 * width :].T.astype(F32)
    gain_one = gains[0]
    gain_two = gains[1]
    conv_taps = gains[2 : 2 + KW]
    out_full = in_full[:, 3 * width : 4 * width]
    in_full = in_full[:, : 3 * width]
    inputs = block_input.reshape(tokens, width).astype(F32)

    def norm_of(value):
        inverse = lax.rsqrt(jnp.mean(value * value, -1, keepdims=True) + EPS)
        return inverse, (value * inverse * gain_one).astype(BF16)

    inv_one, normed_one = norm_of(inputs)
    projected = dot(normed_one, in_full)
    b_part = projected[:, :width]
    c_part = projected[:, width : 2 * width]
    x_part = projected[:, 2 * width :]
    mixed = (b_part * x_part).reshape(micro, rows, width)
    rim = from_behind(mixed[:, rows - (KW - 1) :], 1)
    extended = jnp.concatenate([rim, mixed], 1)
    position = lax.axis_index(EVERY) * rows + lax.iota(jnp.int32, rows)
    masks = [(position[None] - k >= seq_start).astype(F32)[:, :, None] for k in range(KW)]
    conv_out = jnp.zeros_like(mixed)
    for k in range(KW):
        low = KW - 1 - k
        conv_out = conv_out + conv_taps[k] * extended[:, low : low + rows] * masks[k]
    conv_out = conv_out.reshape(tokens, width)
    gated = (c_part * conv_out).astype(BF16)
    resid = inputs + dot(gated, out_full)
    inv_two = lax.rsqrt(jnp.mean(resid * resid, -1, keepdims=True) + EPS)
    normed_two = (resid * inv_two * gain_two).astype(BF16)

    moved = fetch(normed_two, "x")
    hidden = [None] * n_x
    grad_wide = [None] * n_x
    grad_back = [None] * n_x
    for d in (1, 3, 2, 0):
        pre = dot(moved[d] if d else after(moved[d], grad_back[2]), wide)
        gate_pre = pre[:, :share]
        up_pre = pre[:, share:]
        sigma = jax.nn.sigmoid(gate_pre)
        hidden[d] = (gate_pre * sigma * up_pre).astype(BF16)
        grad_hidden = dot(grad_moved[d], down, BACK_DIMS)
        grad_gate = (grad_hidden * up_pre * sigma * (1.0 + gate_pre * (1.0 - sigma))).astype(BF16)
        grad_up = (grad_hidden * gate_pre * sigma).astype(BF16)
        grad_wide[d] = jnp.concatenate([grad_gate, grad_up], 1)
        grad_back[d] = dot(grad_wide[d], wide, BACK_DIMS)
    grad_normed = grad_back[0]
    for d in (1, 3, 2):
        grad_normed = grad_normed + shift(grad_back[d].astype(BF16), "x", -d).astype(F32)

    moved, grad_wide, hidden, term_grads = after(
        (moved, grad_wide, hidden, grad_moved), grad_back
    )
    wide_term = weight_term(moved, grad_wide, 384, 0, 2 * share // 384)
    down_term = weight_term(hidden, term_grads, 512, 0, width // 512)
    gated_moved = fetch(after(gated, grad_normed), "x")
    wide_term, down_term, gated_moved = after((wide_term, down_term, gated_moved), gated_moved)
    down_term = down_term.reshape(GROUP_SIZE, piece, width)
    rest = down_term[:, owned:].reshape(GROUP_SIZE, piece - owned, width // 128, 128)
    ffn_term = jnp.concatenate(
        [
            wide_term,
            down_term[:, :owned].reshape(-1, width),
            rest.swapaxes(1, 2).reshape(-1, 128),
        ],
        1,
    )
    grad_normed = after(grad_normed, ffn_term)
    ffn_sum = lax.psum_scatter(ffn_term, GROUP, scatter_dimension=0, tiled=True)

    grad_out = grad_low.astype(F32)
    ffn_gain_term = jnp.sum(grad_normed * resid * inv_two, 0)
    hat_two = grad_normed * gain_two
    grad_resid = (
        grad_out
        + inv_two * hat_two
        - resid * inv_two**3 * jnp.mean(hat_two * resid, -1, keepdims=True)
    )
    grad_branch = grad_resid.astype(BF16)
    grad_gated = dot(grad_branch, out_full, BACK_DIMS)
    grad_c = grad_gated * conv_out
    grad_conv = (grad_gated * c_part).reshape(micro, rows, width)
    tap_terms = []
    grad_extended = jnp.zeros_like(extended)
    for k in range(KW):
        low = KW - 1 - k
        masked = grad_conv * masks[k]
        tap_terms.append(jnp.sum(masked * extended[:, low : low + rows], (0, 1)))
        grad_extended = grad_extended + jnp.pad(
            masked * conv_taps[k], ((0, 0), (low, k), (0, 0))
        )
    incoming = from_behind(grad_extended[:, : KW - 1], -1)
    grad_mixed = grad_extended[:, KW - 1 :] + jnp.pad(
        incoming, ((0, 0), (rows - (KW - 1), 0), (0, 0))
    )
    grad_mixed = grad_mixed.reshape(tokens, width)
    grad_projected = jnp.concatenate([grad_mixed * x_part, grad_c, grad_mixed * b_part], 1).astype(
        BF16
    )

    def columns_of(d):
        return jnp.concatenate(
            [block_of(grad_projected, "x", d, 1), block_of(grad_branch, "x", d, 1)], 1
        )

    taken = [columns_of(0)] + [shift(columns_of(d), "x", d) for d in range(1, n_x)]
    ffn_sum = scatter_sum(ffn_sum, "y", 0).astype(BF16)
    hidden = after(hidden, grad_projected)
    block_parts = [resid + dot(hidden[0], down)]
    for d in range(1, n_x):
        block_parts.append(dot(hidden[d], down).astype(BF16))
    taken, block_parts = after((taken, block_parts), block_parts)
    grad_first = dot(grad_projected, in_full, BACK_DIMS)
    norm_term = jnp.sum(grad_first * inputs * inv_one, 0)
    hat_one = grad_first * gain_one
    grad_input = (
        grad_resid
        + inv_one * hat_one
        - inputs * inv_one**3 * jnp.mean(hat_one * inputs, -1, keepdims=True)
    )
    normed_moved = [normed_one] + [
        norm_of(value.astype(F32))[1] for value in input_moved[1:]
    ]
    in_part = 3 * width // n_x
    out_part = width // n_x
    in_term = weight_term(normed_moved, taken, out_part, 0, 3)
    out_term = weight_term(gated_moved, taken, out_part, 3, 1)
    small = jnp.pad(
        jnp.stack([norm_term, ffn_gain_term] + tap_terms, 0), ((0, 128 - 2 - KW), (0, 0))
    )
    branch_term = jnp.concatenate([in_term, out_term, small.T.astype(BF16)], 1)
    branch_sum = branch_term.reshape(lax.axis_size("z"), 2, owned, -1)
    branch_sum = scatter_sum(branch_sum, "core", 1).astype(BF16)
    block_parts = block_parts[:1] + [
        shift(block_parts[d], "x", -d) for d in range(1, n_x)
    ]
    branch_sum, ffn_sum, block_parts = after((branch_sum, ffn_sum, block_parts), ffn_sum)
    ffn_sum = lax.all_gather(ffn_sum, ("y", "x"), axis=0)
    branch_sum = scatter_sum(branch_sum, "z", 0)
    branch_sum = branch_sum.astype(BF16).reshape(owned, -1)

    ffn_sum = ffn_sum.reshape(lax.axis_size("y"), n_x, *ffn_sum.shape[1:])
    gate_grad, up_grad, down_grad = unpack(ffn_sum, hidden_width, width)

    branch_sum = gather(scatter_sum(branch_sum, "y", 0).astype(BF16), "y", 0)
    parts = fetch(branch_sum, "x")

    block_out = sum(part.astype(F32) for part in block_parts)
    result = block_out.astype(BF16)

    in_grad = place([part[:, :in_part] for part in parts], "x", 1, F32)
    out_grad = place([part[:, in_part : in_part + out_part] for part in parts], "x", 1, F32)
    gain_grads = sum(part[:, in_part + out_part :].astype(F32) for part in parts).T
    return (
        result.reshape(micro, rows, width),
        grad_input.reshape(micro, rows, width),
        gain_grads[0],
        in_grad,
        gain_grads[2 : 2 + KW],
        out_grad,
        gain_grads[1],
        gate_grad,
        up_grad,
        down_grad,
    )


def solution(mesh):
    fine = Mesh(mesh.devices.reshape(4, 4, 4, 2), EVERY)
    token = P(None, EVERY, None)
    owner = P(GROUP, None)
    return jax.shard_map(
        shards,
        mesh=fine,
        in_specs=(
            token,
            P(None, EVERY),
            P(GROUP),
            owner,
            P(None, GROUP),
            owner,
            P(GROUP),
            owner,
            owner,
            owner,
            token,
        ),
        out_specs=(
            token,
            token,
            P(GROUP),
            owner,
            P(None, GROUP),
            owner,
            P(GROUP),
            owner,
            owner,
            owner,
        ),
        check_vma=False,
    )
```

```python
import jax
import jax.numpy as jnp
from jax import lax
from jax.experimental import pallas as pl
from jax.experimental.pallas import tpu as pltpu
from jax.sharding import Mesh, PartitionSpec as P

KW = 3
EPS = 1e-05
GROUP = ("z", "core")
EVERY = ("y", "x", "z", "core")
GROUP_SIZE = 8
CONTRACT = (((0,), (0,)), ((), ()))
BACK_DIMS = (((1,), (1,)), ((), ()))
F32 = jnp.float32
BF16 = jnp.bfloat16


def dot(a, b, dims=(((1,), (0,)), ((), ()))):
    return lax.dot_general(a, b, dims, preferred_element_type=F32)


def shift(value, axis, distance):
    size = lax.axis_size(axis)
    return lax.ppermute(value, axis, [(i, (i + distance) % size) for i in range(size)])


def from_behind(block, distance):
    size = lax.axis_size(EVERY)
    route = [(i - distance, i) for i in range(size) if 0 <= i - distance < size]
    return lax.ppermute(block, EVERY, route)


def fetch(value, axis):
    return [value] + [shift(value, axis, d) for d in range(1, lax.axis_size(axis))]


def place(pieces, axis, dim, dtype):
    size = lax.axis_size(axis)
    here = lax.axis_index(axis)
    width = pieces[0].shape[dim]
    shape = list(pieces[0].shape)
    shape[dim] = width * size
    out = jnp.zeros(shape, dtype)
    for d, piece in enumerate(pieces):
        start = lax.rem(here - d + size, size) * width
        out = lax.dynamic_update_slice_in_dim(out, piece.astype(dtype), start, dim)
    return out


def gather(value, axis, dim, dtype=BF16):
    return place(fetch(value, axis), axis, dim, dtype)


def scatter_sum(value, axis, dim):
    size = lax.axis_size(axis)
    here = lax.axis_index(axis)
    width = value.shape[dim] // size

    def block(d):
        start = lax.rem(here + d, size) * width
        return lax.dynamic_slice_in_dim(value, start, width, dim)

    total = block(0).astype(F32)
    for d in range(1, size):
        total = total + shift(block(d).astype(BF16), axis, d).astype(F32)
    return total


def term_kernel(*refs):
    count = (len(refs) - 2) // 2
    lefts, rights = refs[:count], refs[count : 2 * count]
    out, turned = refs[2 * count :]
    rows = lefts[0].shape[0]

    @pl.when(pl.program_id(0) == 0)
    def _():
        for i, left in enumerate(lefts):
            turned[:, i * rows : (i + 1) * rows] = left[...].T

    total = dot(turned[:, :rows], rights[0][...])
    for i in range(1, count):
        total = total + dot(turned[:, i * rows : (i + 1) * rows], rights[i][...])
    out[...] = total.astype(out.dtype)


def weight_term(lefts, rights, tile, skip, tiles):
    rows, tall = lefts[0].shape
    wide = tile * tiles
    count = len(lefts)
    return pl.pallas_call(
        term_kernel,
        grid=(tiles,),
        in_specs=[pl.BlockSpec((rows, tall), lambda i: (0, 0))] * count
        + [pl.BlockSpec((rows, tile), lambda i: (0, i + skip))] * count,
        out_specs=pl.BlockSpec((tall, tile), lambda i: (0, i)),
        out_shape=jax.ShapeDtypeStruct((tall, wide), BF16),
        scratch_shapes=[pltpu.VMEM((tall, rows * count), BF16)],
        compiler_params=pltpu.CompilerParams(
            vmem_limit_bytes=16 * 1024 * 1024, dimension_semantics=("arbitrary",)
        ),
        cost_estimate=pl.CostEstimate(
            flops=2 * count * rows * tall * wide,
            bytes_accessed=2 * (count * rows * (tall + wide) + tall * wide),
            transcendentals=0,
        ),
    )(*lefts, *rights)


def unpack_kernel(source, gate, up, down):
    n_y, n_x, strip, _ = source.shape
    rows = n_y * strip
    n_group = GROUP_SIZE
    share = gate.shape[1] // n_x
    piece = share // n_group
    width = down.shape[1]
    for half, out in enumerate((gate, up)):
        for j in range(n_group):
            low = half * share + j * piece
            for y in range(n_y):
                parts = [source[y, x, :, low : low + piece].astype(F32) for x in range(n_x)]
                out[
                    y * strip : (y + 1) * strip, j * n_x * piece : (j + 1) * n_x * piece
                ] = jnp.concatenate(parts, 1)
    rest = piece - rows
    for x in range(n_x):
        top = x * piece
        for y in range(n_y):
            main = source[y, x, :, 2 * share : 2 * share + width]
            down[top + y * strip : top + (y + 1) * strip] = main.astype(F32)
        for q in range(rows // rest):
            y, low = divmod(q * rest, strip)
            block = source[y, x, low : low + rest, 2 * share + width :]
            down[top + rows : top + piece, q * 128 : (q + 1) * 128] = block.astype(F32)


def unpack(source, hidden_width, width):
    n_y, n_x, strip, packed = source.shape
    rows = n_y * strip
    shapes = [(rows, hidden_width), (rows, hidden_width), (hidden_width // GROUP_SIZE, width)]
    return pl.pallas_call(
        unpack_kernel,
        out_shape=[jax.ShapeDtypeStruct(shape, F32) for shape in shapes],
        compiler_params=pltpu.CompilerParams(vmem_limit_bytes=20 * 1024 * 1024),
        cost_estimate=pl.CostEstimate(
            flops=0, bytes_accessed=6 * n_x * rows * packed, transcendentals=0
        ),
    )(source)


def after(value, *others):
    return lax.optimization_barrier((value, others))[0]


def block_of(value, axis, distance, dim):
    size = lax.axis_size(axis)
    width = value.shape[dim] // size
    start = lax.rem(lax.axis_index(axis) + distance, size) * width
    return lax.dynamic_slice_in_dim(value, start, width, dim)


def shards(
    block_input,
    seq_start,
    norm_gain,
    in_weight,
    conv_weight,
    out_weight,
    ffn_gain,
    gate_weight,
    up_weight,
    down_weight,
    cotangent,
):
    micro, rows, width = block_input.shape
    owned, hidden_width = gate_weight.shape
    n_x = lax.axis_size("x")
    x_here = lax.axis_index("x")
    tokens = micro * rows
    share = hidden_width // n_x
    piece = share // GROUP_SIZE

    columns = jnp.pad(
        jnp.concatenate([norm_gain[None], ffn_gain[None], conv_weight], 0), ((0, 128 - 2 - KW), (0, 0))
    ).T
    in_full = lax.all_gather(
        jnp.concatenate([in_weight, out_weight, columns], 1), GROUP, axis=0, tiled=True
    )
    down_strip = block_of(block_of(down_weight, "x", 0, 0), "y", 0, 1)
    joined = place([part[None] for part in fetch(down_strip, "z")], "z", 0, BF16)
    joined = place(fetch(joined, "y"), "y", 2, BF16)

    grad_low = cotangent.reshape(tokens, width)
    grad_moved = fetch(grad_low, "x")
    input_moved = fetch(block_input.reshape(tokens, width), "x")

    def quarter(weight):
        split = weight.reshape(owned, GROUP_SIZE, n_x, piece)
        return lax.dynamic_index_in_dim(split, x_here, 2, False).reshape(owned, share)

    wide = jnp.concatenate([quarter(gate_weight), quarter(up_weight)], 1)
    wide = lax.all_gather(
        after(wide, in_full, joined, grad_moved), GROUP, axis=0, tiled=True
    )
    cores = fetch(joined, "core")
    down = place([part[:, None] for part in cores], "core", 1, BF16).reshape(-1, width)

    gains = in_full[:, 4 * width :].T.astype(F32)
    gain_one = gains[0]
    gain_two = gains[1]
    conv_taps = gains[2 : 2 + KW]
    out_full = in_full[:, 3 * width : 4 * width]
    in_full = in_full[:, : 3 * width]
    inputs = block_input.reshape(tokens, width).astype(F32)

    def norm_of(value):
        inverse = lax.rsqrt(jnp.mean(value * value, -1, keepdims=True) + EPS)
        return inverse, (value * inverse * gain_one).astype(BF16)

    inv_one, normed_one = norm_of(inputs)
    projected = dot(normed_one, in_full)
    b_part = projected[:, :width]
    c_part = projected[:, width : 2 * width]
    x_part = projected[:, 2 * width :]
    mixed = (b_part * x_part).reshape(micro, rows, width)
    rim = from_behind(mixed[:, rows - (KW - 1) :], 1)
    extended = jnp.concatenate([rim, mixed], 1)
    position = lax.axis_index(EVERY) * rows + lax.iota(jnp.int32, rows)
    masks = [(position[None] - k >= seq_start).astype(F32)[:, :, None] for k in range(KW)]
    conv_out = jnp.zeros_like(mixed)
    for k in range(KW):
        low = KW - 1 - k
        conv_out = conv_out + conv_taps[k] * extended[:, low : low + rows] * masks[k]
    conv_out = conv_out.reshape(tokens, width)
    gated = (c_part * conv_out).astype(BF16)
    resid = inputs + dot(gated, out_full)
    inv_two = lax.rsqrt(jnp.mean(resid * resid, -1, keepdims=True) + EPS)
    normed_two = (resid * inv_two * gain_two).astype(BF16)

    normed_two, input_moved = after((normed_two, input_moved), input_moved)
    moved = fetch(normed_two, "x")
    hidden = [None] * n_x
    grad_wide = [None] * n_x
    grad_back = [None] * n_x
    for d in (1, 3, 2, 0):
        pre = dot(moved[d] if d else after(moved[d], grad_back[2]), wide)
        gate_pre = pre[:, :share]
        up_pre = pre[:, share:]
        sigma = jax.nn.sigmoid(gate_pre)
        hidden[d] = (gate_pre * sigma * up_pre).astype(BF16)
        grad_hidden = dot(grad_moved[d], down, BACK_DIMS)
        grad_gate = (grad_hidden * up_pre * sigma * (1.0 + gate_pre * (1.0 - sigma))).astype(BF16)
        grad_up = (grad_hidden * gate_pre * sigma).astype(BF16)
        grad_wide[d] = jnp.concatenate([grad_gate, grad_up], 1)
        grad_back[d] = dot(grad_wide[d], wide, BACK_DIMS)
    grad_normed = grad_back[0]
    for d in (1, 3, 2):
        grad_normed = grad_normed + shift(grad_back[d].astype(BF16), "x", -d).astype(F32)

    moved, grad_wide, hidden, term_grads = after(
        (moved, grad_wide, hidden, grad_moved), grad_back
    )
    wide_term = weight_term(moved, grad_wide, 384, 0, 2 * share // 384)
    down_term = weight_term(hidden, term_grads, 512, 0, width // 512)
    gated_moved = fetch(after(gated, grad_normed), "x")
    wide_term, down_term, gated_moved = after((wide_term, down_term, gated_moved), gated_moved)
    down_term = down_term.reshape(GROUP_SIZE, piece, width)
    rest = down_term[:, owned:].reshape(GROUP_SIZE, piece - owned, width // 128, 128)
    ffn_term = jnp.concatenate(
        [
            wide_term,
            down_term[:, :owned].reshape(-1, width),
            rest.swapaxes(1, 2).reshape(-1, 128),
        ],
        1,
    )
    grad_normed = after(grad_normed, ffn_term)
    ffn_sum = lax.psum_scatter(ffn_term, GROUP, scatter_dimension=0, tiled=True)

    grad_out = grad_low.astype(F32)
    ffn_gain_term = jnp.sum(grad_normed * resid * inv_two, 0)
    hat_two = grad_normed * gain_two
    grad_resid = (
        grad_out
        + inv_two * hat_two
        - resid * inv_two**3 * jnp.mean(hat_two * resid, -1, keepdims=True)
    )
    grad_branch = grad_resid.astype(BF16)
    grad_gated = dot(grad_branch, out_full, BACK_DIMS)
    grad_c = grad_gated * conv_out
    grad_conv = (grad_gated * c_part).reshape(micro, rows, width)
    tap_terms = []
    grad_extended = jnp.zeros_like(extended)
    for k in range(KW):
        low = KW - 1 - k
        masked = grad_conv * masks[k]
        tap_terms.append(jnp.sum(masked * extended[:, low : low + rows], (0, 1)))
        grad_extended = grad_extended + jnp.pad(
            masked * conv_taps[k], ((0, 0), (low, k), (0, 0))
        )
    incoming = from_behind(grad_extended[:, : KW - 1], -1)
    grad_mixed = grad_extended[:, KW - 1 :] + jnp.pad(
        incoming, ((0, 0), (rows - (KW - 1), 0), (0, 0))
    )
    grad_mixed = grad_mixed.reshape(tokens, width)
    grad_projected = jnp.concatenate([grad_mixed * x_part, grad_c, grad_mixed * b_part], 1).astype(
        BF16
    )

    def columns_of(d):
        return jnp.concatenate(
            [block_of(grad_projected, "x", d, 1), block_of(grad_branch, "x", d, 1)], 1
        )

    taken = [columns_of(0)] + [shift(columns_of(d), "x", d) for d in range(1, n_x)]
    ffn_sum = scatter_sum(ffn_sum, "y", 0).astype(BF16)
    hidden = after(hidden, grad_projected)
    block_parts = [resid + dot(hidden[0], down)]
    for d in range(1, n_x):
        block_parts.append(dot(hidden[d], down).astype(BF16))
    taken, block_parts = after((taken, block_parts), block_parts)
    grad_first = dot(grad_projected, in_full, BACK_DIMS)
    norm_term = jnp.sum(grad_first * inputs * inv_one, 0)
    hat_one = grad_first * gain_one
    grad_input = (
        grad_resid
        + inv_one * hat_one
        - inputs * inv_one**3 * jnp.mean(hat_one * inputs, -1, keepdims=True)
    )
    normed_moved = [normed_one] + [
        norm_of(value.astype(F32))[1] for value in input_moved[1:]
    ]
    in_part = 3 * width // n_x
    out_part = width // n_x
    in_term = weight_term(normed_moved, taken, out_part, 0, 3)
    out_term = weight_term(gated_moved, taken, out_part, 3, 1)
    small = jnp.pad(
        jnp.stack([norm_term, ffn_gain_term] + tap_terms, 0), ((0, 128 - 2 - KW), (0, 0))
    )
    branch_term = jnp.concatenate([in_term, out_term, small.T.astype(BF16)], 1)
    branch_sum = branch_term.reshape(lax.axis_size("z"), 2, owned, -1)
    branch_sum = scatter_sum(branch_sum, "core", 1).astype(BF16)
    block_parts = block_parts[:1] + [
        shift(block_parts[d], "x", -d) for d in range(1, n_x)
    ]
    branch_sum, ffn_sum, block_parts = after((branch_sum, ffn_sum, block_parts), ffn_sum)
    ffn_sum = lax.all_gather(ffn_sum, ("y", "x"), axis=0)
    branch_sum = scatter_sum(branch_sum, "z", 0)
    branch_sum = branch_sum.astype(BF16).reshape(owned, -1)

    ffn_sum = ffn_sum.reshape(lax.axis_size("y"), n_x, *ffn_sum.shape[1:])
    gate_grad, up_grad, down_grad = unpack(ffn_sum, hidden_width, width)

    branch_sum = gather(scatter_sum(branch_sum, "y", 0).astype(BF16), "y", 0)
    parts = fetch(branch_sum, "x")

    block_out = sum(part.astype(F32) for part in block_parts)
    result = block_out.astype(BF16)

    in_grad = place([part[:, :in_part] for part in parts], "x", 1, F32)
    out_grad = place([part[:, in_part : in_part + out_part] for part in parts], "x", 1, F32)
    gain_grads = sum(part[:, in_part + out_part :].astype(F32) for part in parts).T
    return (
        result.reshape(micro, rows, width),
        grad_input.reshape(micro, rows, width),
        gain_grads[0],
        in_grad,
        gain_grads[2 : 2 + KW],
        out_grad,
        gain_grads[1],
        gate_grad,
        up_grad,
        down_grad,
    )


def solution(mesh):
    fine = Mesh(mesh.devices.reshape(4, 4, 4, 2), EVERY)
    token = P(None, EVERY, None)
    owner = P(GROUP, None)
    return jax.shard_map(
        shards,
        mesh=fine,
        in_specs=(
            token,
            P(None, EVERY),
            P(GROUP),
            owner,
            P(None, GROUP),
            owner,
            P(GROUP),
            owner,
            owner,
            owner,
            token,
        ),
        out_specs=(
            token,
            token,
            P(GROUP),
            owner,
            P(None, GROUP),
            owner,
            P(GROUP),
            owner,
            owner,
            owner,
        ),
        check_vma=False,
    )
```
